32 devices in a mesh: row: 8 (over y, x, core), col: 4 (over z).
Axes of the slice: x: 2, y: 2, z: 4, core: 2. Of those that a mesh axis runs over, the one named last changes fastest.
Arguments:
- tokens: bfloat16 [512, 8192], P('col', 'row'), may hold values from -6 to 6
- cotangent: bfloat16 [512, 8192], P('col', 'row'), may hold values from -1.5 to 1.5
- gate_weight: bfloat16 [8192, 14336], P('row', 'col'), may hold values from -0.0625 to 0.0625
- up_weight: bfloat16 [8192, 14336], P('row', 'col'), may hold values from -0.0625 to 0.0625
- down_weight: bfloat16 [14336, 8192], P('col', 'row'), may hold values from -0.046875 to 0.046875
Outputs:
- layer_output: bfloat16 [512, 8192], P('col', 'row')
- input_grad: bfloat16 [512, 8192], P('col', 'row')
- gate_weight_grad: bfloat16 [8192, 14336], P('row', 'col')
- up_weight_grad: bfloat16 [8192, 14336], P('row', 'col')
- down_weight_grad: bfloat16 [14336, 8192], P('col', 'row')
The draws below stay inside these ranges and needn't reach their ends.
All inputs are finite; a program needn't handle non-finite values.
Results may differ from the reference program's by a relative error of at most 0.0049.
Values may be sent and summed in bfloat16 or wider, within the bound.
A program may use at most 192 MiB of HBM per device.

```python
import jax
import jax.numpy as jnp

D = 8192
FF = 14336
TOKENS = 512


def levels(stream_key, extent, split, least, top_value):
    level = 1.0
    for dim, parts in split:
        draws = jax.random.uniform(jax.random.fold_in(jax.random.fold_in(stream_key, 6), dim), (parts,), jnp.float32, least / len(split), top_value / len(split))
        level = level * jnp.repeat(jnp.exp(draws), extent[dim] // parts).reshape((-1,) + (1,) * (len(extent) - 1 - dim))
    return level


def centred(own_key, dims, deviation, bound, shards=(), held_as=jnp.bfloat16):
    factor_of = levels(own_key, dims, shards, -0.22, 0.18) if shards else 1.0
    values = jax.random.normal(own_key, dims, jnp.float32) * deviation * factor_of
    return jnp.minimum(jnp.maximum(values, -bound), bound).astype(held_as)


def setup_inputs(seed: int = 0) -> dict:
    key_of = jax.random.split(jax.random.key(seed), 6)
    tokens = centred(key_of[0], (TOKENS, D), 1.0, 6.0, ((0, 4), (1, 8)))
    cotangent = centred(key_of[1], (TOKENS, D), 0.25, 1.5, ((0, 4), (1, 8)))
    gate_weight = centred(key_of[2], (D, FF), D ** -0.5, 0.0625, ((0, 8), (1, 4)))
    up_weight = centred(key_of[3], (D, FF), D ** -0.5, 0.0625, ((0, 8), (1, 4)))
    down_weight = centred(key_of[4], (FF, D), FF ** -0.5, 0.046875, ((0, 4), (1, 8)))
    return dict(tokens=tokens, cotangent=cotangent, gate_weight=gate_weight, up_weight=up_weight, down_weight=down_weight)


def reference(tokens, cotangent, gate_weight, up_weight, down_weight):
    gate_sum = jnp.dot(tokens, gate_weight, preferred_element_type=jnp.float32)
    up_sum = jnp.dot(tokens, up_weight, preferred_element_type=jnp.float32)
    sigmoid_gate = jax.nn.sigmoid(gate_sum)
    silu_gate = gate_sum * sigmoid_gate
    hidden = (silu_gate * up_sum).astype(jnp.bfloat16)
    layer_output = jnp.dot(hidden, down_weight, preferred_element_type=jnp.float32).astype(jnp.bfloat16)
    hidden_grad = jnp.dot(cotangent, down_weight.T, preferred_element_type=jnp.float32)
    down_weight_grad = jnp.dot(hidden.T, cotangent, preferred_element_type=jnp.float32).astype(jnp.bfloat16)
    silu_slope = sigmoid_gate * (1.0 + gate_sum * (1.0 - sigmoid_gate))
    gate_grad = (hidden_grad * up_sum * silu_slope).astype(jnp.bfloat16)
    up_grad = (hidden_grad * silu_gate).astype(jnp.bfloat16)
    input_sum = jnp.dot(gate_grad, gate_weight.T, preferred_element_type=jnp.float32) + jnp.dot(up_grad, up_weight.T, preferred_element_type=jnp.float32)
    input_grad = input_sum.astype(jnp.bfloat16)
    gate_weight_grad = jnp.dot(tokens.T, gate_grad, preferred_element_type=jnp.float32).astype(jnp.bfloat16)
    up_weight_grad = jnp.dot(tokens.T, up_grad, preferred_element_type=jnp.float32).astype(jnp.bfloat16)
    return (layer_output, input_grad, gate_weight_grad, up_weight_grad, down_weight_grad)
```

```python
import jax
import jax.numpy as jnp
from jax import lax
from jax.sharding import PartitionSpec as P

F32 = jnp.float32
BF16 = jnp.bfloat16


def contract_last(left, right):
    return lax.dot_general(left, right, (((1,), (1,)), ((), ())), preferred_element_type=F32)


def contract_first(left, right):
    return lax.dot_general(left, right, (((0,), (0,)), ((), ())), preferred_element_type=F32)


def solution(mesh):
    rows, cols = mesh.shape["row"], mesh.shape["col"]
    bits = rows.bit_length() - 1

    def swap(block, bit):
        return lax.ppermute(block, "row", [(i, i ^ (1 << bit)) for i in range(rows)])

    def shift(block, by):
        return lax.ppermute(block, "col", [(i, (i + by) % cols) for i in range(cols)])

    def half(block, axis, side):
        return lax.slice_in_dim(block, side, side + 1, axis=axis)

    def blocked(panel):
        return panel.reshape((2,) * bits + (panel.shape[0] // rows, panel.shape[1]))

    def relative(panel):
        me = lax.axis_index("row")
        block = blocked(panel)
        for bit in range(bits):
            block = jnp.where((me >> bit) & 1 == 1, jnp.flip(block, bit), block)
        return block.reshape(panel.shape)

    def local(tokens, cotangent, gate_weight, up_weight, down_weight):
        width = gate_weight.shape[1]
        orders = [list(range(1, bits)), list(range(bits - 1, 0, -1))]
        edge = width // 2 // 128 * 128
        spans = [(0, edge), (edge, width)]

        token_parts, grad_parts = [relative(tokens)], [relative(cotangent)]
        for _ in range(cols - 1):
            token_parts.append(shift(token_parts[-1], 1))
            grad_parts.append(shift(grad_parts[-1], 1))

        panels, out_sum, in_sum = [], None, None
        for step in range(cols):
            part, grad = token_parts[step], grad_parts[step]
            sums = [
                blocked(contract_last(grad, down_weight)),
                blocked(jnp.dot(part, gate_weight, preferred_element_type=F32)),
                blocked(jnp.dot(part, up_weight, preferred_element_type=F32)),
            ]
            sent = swap(jnp.concatenate([half(s, 0, 1) for s in sums], axis=-1), 0)
            joined = [
                half(s, 0, 0) + sent[..., i * width : (i + 1) * width] for i, s in enumerate(sums)
            ]
            gathered = []
            for order, (low, high) in zip(orders, spans):
                total = jnp.concatenate([j[..., low:high] for j in joined], axis=-1)
                for bit in order:
                    away = swap(half(total, bit, 1).astype(BF16), bit)
                    total = half(total, bit, 0) + away.astype(F32)
                hidden_grad, own_gate, own_up = jnp.split(total, 3, axis=-1)
                sigmoid_gate = jax.nn.sigmoid(own_gate)
                silu_gate = own_gate * sigmoid_gate
                slope = sigmoid_gate * (1.0 + own_gate * (1.0 - sigmoid_gate))
                own = jnp.concatenate(
                    [
                        (silu_gate * own_up).astype(BF16),
                        (hidden_grad * own_up * slope).astype(BF16),
                        (hidden_grad * silu_gate).astype(BF16),
                    ],
                    axis=-1,
                )
                for bit in reversed(order):
                    own = jnp.concatenate([own, swap(own, bit)], axis=bit)
                gathered.append(own)
            kinds = [jnp.split(g, 3, axis=-1) for g in gathered]
            mine = [jnp.concatenate([k[i] for k in kinds], axis=-1) for i in range(3)]
            other = swap(jnp.concatenate(gathered, axis=-1), 0)
            theirs, start = [[], [], []], 0
            for low, high in spans:
                for i in range(3):
                    theirs[i].append(other[..., start : start + high - low])
                    start += high - low
            full = [
                jnp.concatenate([m, jnp.concatenate(t, axis=-1)], axis=0).reshape(-1, width)
                for m, t in zip(mine, theirs)
            ]
            panels.append(full)
            hidden, gate_grad, up_grad = full
            in_part = contract_last(gate_grad, gate_weight) + contract_last(up_grad, up_weight)
            out_part = jnp.dot(hidden, down_weight, preferred_element_type=F32)
            if step == 0:
                out_sum, in_sum = out_part, in_part
            else:
                in_sum = in_sum + shift(in_part.astype(BF16), -step).astype(F32)
                out_sum = out_sum + shift(out_part.astype(BF16), -step).astype(F32)

        token_panel = jnp.concatenate(token_parts, axis=0)
        grad_panel = jnp.concatenate(grad_parts, axis=0)
        hidden, gate_grad, up_grad = (
            jnp.concatenate([p[i] for p in panels], axis=0) for i in range(3)
        )
        return (
            relative(out_sum.astype(BF16)),
            relative(in_sum.astype(BF16)),
            contract_first(token_panel, gate_grad).astype(BF16),
            contract_first(token_panel, up_grad).astype(BF16),
            contract_first(hidden, grad_panel).astype(BF16),
        )

    return jax.shard_map(
        local,
        mesh=mesh,
        in_specs=(P("col", "row"), P("col", "row"), P("row", "col"), P("row", "col"), P("col", "row")),
        out_specs=(P("col", "row"), P("col", "row"), P("row", "col"), P("row", "col"), P("col", "row")),
        check_vma=False,
    )
```

```python
import jax
import jax.numpy as jnp
from jax import lax
from jax.sharding import PartitionSpec as P

F32 = jnp.float32
BF16 = jnp.bfloat16


def contract_last(left, right):
    return lax.dot_general(left, right, (((1,), (1,)), ((), ())), preferred_element_type=F32)


def contract_first(left, right):
    return lax.dot_general(left, right, (((0,), (0,)), ((), ())), preferred_element_type=F32)


def solution(mesh):
    rows, cols = mesh.shape["row"], mesh.shape["col"]
    bits = rows.bit_length() - 1

    def swap(block, bit):
        return lax.ppermute(block, "row", [(i, i ^ (1 << bit)) for i in range(rows)])

    def shift(block, by):
        return lax.ppermute(block, "col", [(i, (i + by) % cols) for i in range(cols)])

    def half(block, axis, side):
        return lax.slice_in_dim(block, side, side + 1, axis=axis)

    def blocked(panel):
        return panel.reshape((2,) * bits + (panel.shape[0] // rows, panel.shape[1]))

    def relative(panel):
        me = lax.axis_index("row")
        block = blocked(panel)
        for bit in range(bits):
            block = jnp.where((me >> bit) & 1 == 1, jnp.flip(block, bit), block)
        return block.reshape(panel.shape)

    def local(tokens, cotangent, gate_weight, up_weight, down_weight):
        width = gate_weight.shape[1]
        orders = [list(range(1, bits)), list(range(bits - 1, 0, -1))]
        edge = width // 2 // 128 * 128
        spans = [(0, edge), (edge, width)]

        tokens_at, grads_at = {0: relative(tokens)}, {0: relative(cotangent)}
        live, last = {}, cols - 1

        def products(k):
            part, grad = tokens_at[k], grads_at[k]
            sums = [
                blocked(contract_last(grad, down_weight)),
                blocked(jnp.dot(part, gate_weight, preferred_element_type=F32)),
                blocked(jnp.dot(part, up_weight, preferred_element_type=F32)),
            ]
            live["core_out", k] = jnp.concatenate([half(s, 0, 1) for s in sums], axis=-1)
            live["core_keep", k] = [half(s, 0, 0) for s in sums]

        def core_sum(k):
            live["core_in", k] = swap(live.pop(("core_out", k)), 0)

        def reduce_stage(k, stage):
            if stage == 0:
                sent, keep = live.pop(("core_in", k)), live.pop(("core_keep", k))
                joined = [s + sent[..., i * width : (i + 1) * width] for i, s in enumerate(keep)]
                totals = [
                    jnp.concatenate([j[..., low:high] for j in joined], axis=-1)
                    for low, high in spans
                ]
            else:
                totals = merged(k)
            arrived, kept = [], []
            for order, total in zip(orders, totals):
                bit = order[stage]
                arrived.append(swap(half(total, bit, 1).astype(BF16), bit))
                kept.append(half(total, bit, 0))
            live["arrived", k], live["kept", k] = arrived, kept

        def merged(k):
            return [
                a.astype(F32) + b for a, b in zip(live.pop(("arrived", k)), live.pop(("kept", k)))
            ]

        def activate(total):
            hidden_grad, own_gate, own_up = jnp.split(total, 3, axis=-1)
            sigmoid_gate = jax.nn.sigmoid(own_gate)
            silu_gate = own_gate * sigmoid_gate
            slope = sigmoid_gate * (1.0 + own_gate * (1.0 - sigmoid_gate))
            return jnp.concatenate(
                [
                    (silu_gate * own_up).astype(BF16),
                    (hidden_grad * own_up * slope).astype(BF16),
                    (hidden_grad * silu_gate).astype(BF16),
                ],
                axis=-1,
            )

        def gather_stage(k, stage):
            owns = [activate(t) for t in merged(k)] if stage == 0 else collected(k)
            live["own", k] = owns
            live["came", k] = [
                swap(own, order[-1 - stage]) for own, order in zip(owns, orders)
            ]
            live["axis", k] = stage

        def collected(k):
            stage = live.pop(("axis", k))
            return [
                jnp.concatenate([own, came], axis=order[-1 - stage])
                for own, came, order in zip(live.pop(("own", k)), live.pop(("came", k)), orders)
            ]

        def core_gather(k):
            owns = collected(k)
            live["mine", k] = owns
            live["other", k] = [swap(own, 0) for own in owns]

        def outputs(k):
            mine, other = live.pop(("mine", k)), live.pop(("other", k))
            mine = [jnp.split(m, 3, axis=-1) for m in mine]
            other = [jnp.split(o, 3, axis=-1) for o in other]
            full = [
                jnp.concatenate(
                    [
                        jnp.concatenate([m[i] for m in mine], axis=-1),
                        jnp.concatenate([o[i] for o in other], axis=-1),
                    ],
                    axis=0,
                ).reshape(-1, width)
                for i in range(3)
            ]
            live["full", k] = full
            hidden, gate_grad, up_grad = full
            in_part = contract_last(gate_grad, gate_weight) + contract_last(up_grad, up_weight)
            out_part = jnp.dot(hidden, down_weight, preferred_element_type=F32)
            kind = F32 if k == 0 else BF16
            live["parts", k] = [out_part.astype(kind), in_part.astype(kind)]

        def send_outputs(k):
            if k:
                live["back", k] = [shift(p, -k) for p in live.pop(("parts", k))]

        def next_tokens(k):
            if k <= last:
                tokens_at[k] = shift(tokens_at[k - 1], 1)
                grads_at[k] = shift(grads_at[k - 1], 1)

        def settle():
            nonlocal live, tokens_at, grads_at
            axes = {key: live.pop(key) for key in [key for key in live if key[0] == "axis"]}
            names = list(live)
            values, t, g = lax.optimization_barrier(
                ([live[n] for n in names], list(tokens_at.values()), list(grads_at.values()))
            )
            live = dict(zip(names, values)) | axes
            tokens_at, grads_at = dict(enumerate(t)), dict(enumerate(g))

        stages = bits - 1
        chunk = lambda k: 2 + stages * k
        plan = {}

        def at(slot, work, *args):
            plan.setdefault(slot, []).append((work, args))

        for k in range(cols):
            first = chunk(k)
            for stage in range(stages):
                at(first + stage, reduce_stage, k, stage)
                at(first + stages + stage, gather_stage, k, stage)
            at(first - 1, core_sum, k)
            at(first - 2, products, k)
            at(first + 2 * stages, core_gather, k)
            at(first + 2 * stages + 1, outputs, k)
            at(first + 2 * stages + 2, send_outputs, k)
            if k:
                at(min(k - 1, first - 3), next_tokens, k)
        rank = [next_tokens, core_sum, gather_stage, reduce_stage, core_gather, send_outputs, products, outputs]
        for slot in range(max(plan) + 1):
            for work, args in sorted(plan.get(slot, []), key=lambda w: rank.index(w[0])):
                work(*args)
            if slot < max(plan):
                settle()

        out_sum, in_sum = live["parts", 0]
        token_panel = jnp.concatenate([tokens_at[k] for k in range(cols)], axis=0)
        grad_panel = jnp.concatenate([grads_at[k] for k in range(cols)], axis=0)
        hidden, gate_grad, up_grad = (
            jnp.concatenate([live["full", k][i] for k in range(cols)], axis=0) for i in range(3)
        )
        grads = (
            contract_first(token_panel, gate_grad).astype(BF16),
            contract_first(token_panel, up_grad).astype(BF16),
            contract_first(hidden, grad_panel).astype(BF16),
        )
        for k in range(1, cols):
            out_back, in_back = live["back", k]
            out_sum, in_sum = out_sum + out_back.astype(F32), in_sum + in_back.astype(F32)
        return (relative(out_sum.astype(BF16)), relative(in_sum.astype(BF16))) + grads

    return jax.shard_map(
        local,
        mesh=mesh,
        in_specs=(P("col", "row"), P("col", "row"), P("row", "col"), P("row", "col"), P("col", "row")),
        out_specs=(P("col", "row"), P("col", "row"), P("row", "col"), P("row", "col"), P("col", "row")),
        check_vma=False,
    )
```

```python
import jax
import jax.numpy as jnp
from jax import lax
from jax.sharding import PartitionSpec as P

F32 = jnp.float32
BF16 = jnp.bfloat16


def contract_last(left, right):
    return lax.dot_general(left, right, (((1,), (1,)), ((), ())), preferred_element_type=F32)


def contract_first(left, right):
    return lax.dot_general(left, right, (((0,), (0,)), ((), ())), preferred_element_type=F32)


def solution(mesh):
    rows, cols = mesh.shape["row"], mesh.shape["col"]
    bits = rows.bit_length() - 1

    def swap(block, bit):
        return lax.ppermute(block, "row", [(i, i ^ (1 << bit)) for i in range(rows)])

    def shift(block, by):
        return lax.ppermute(block, "col", [(i, (i + by) % cols) for i in range(cols)])

    def half(block, axis, side):
        return lax.slice_in_dim(block, side, side + 1, axis=axis)

    def blocked(panel):
        return panel.reshape((2,) * bits + (panel.shape[0] // rows, panel.shape[1]))

    def relative(panel):
        me = lax.axis_index("row")
        block = blocked(panel)
        for bit in range(bits):
            block = jnp.where((me >> bit) & 1 == 1, jnp.flip(block, bit), block)
        return block.reshape(panel.shape)

    def local(tokens, cotangent, gate_weight, up_weight, down_weight):
        width = gate_weight.shape[1]
        orders = [list(range(1, bits)), list(range(bits - 1, 0, -1))]
        stages, waves, pair = bits - 1, cols // 2, 2
        tokens_at, grads_at = {0: relative(tokens)}, {0: relative(cotangent)}
        for k in range(1, cols):
            grads_at[k] = shift(grads_at[k - 1], 1)
            tokens_at[k] = shift(tokens_at[k - 1], 1)
        live, back = {}, {}
        split = tokens.shape[0] // 2

        def members(w):
            return [pair * w + s for s in range(pair)]

        def products(w):
            def sums(low, high):
                part = jnp.concatenate([tokens_at[k][low:high] for k in members(w)], axis=0)
                grad = jnp.concatenate([grads_at[k][low:high] for k in members(w)], axis=0)
                return [
                    contract_last(grad, down_weight),
                    jnp.dot(part, gate_weight, preferred_element_type=F32),
                    jnp.dot(part, up_weight, preferred_element_type=F32),
                ]

            live["core_in", w] = [swap(s, 0) for s in sums(split, 2 * split)]
            live["core_keep", w] = sums(0, split)

        def partial(w, s, sides):
            def cut(block, done):
                for stage in range(done, len(sides)):
                    block = half(block, orders[s][stage] - 1, sides[stage])
                return block

            shape = (pair,) + (2,) * (bits - 1) + (2 * split // rows, width)
            values = []
            for i in range(3):
                value = cut(live["core_in", w][i].reshape(shape)[s], 0)
                value = value + cut(live["core_keep", w][i].reshape(shape)[s], 0)
                for stage, side in enumerate(sides):
                    if side == 0:
                        came = live["arrived", w, stage][s][..., i * width : (i + 1) * width]
                        value = value + cut(came, stage + 1).astype(F32)
                values.append(value)
            return values

        def reduce_stage(w, stage):
            arrived = []
            for s, order in enumerate(orders):
                sides = [0] * stage + [1]
                sent = [v.astype(BF16) for v in partial(w, s, sides)]
                arrived.append(swap(jnp.concatenate(sent, axis=-1), order[stage]))
            live["arrived", w, stage] = arrived

        def activated(w):
            owns = [activate(partial(w, s, [0] * stages)) for s in range(pair)]
            for name in [("core_in", w), ("core_keep", w)] + [("arrived", w, q) for q in range(stages)]:
                live.pop(name)
            return owns

        def activate(total):
            hidden_grad, own_gate, own_up = total
            sigmoid_gate = jax.nn.sigmoid(own_gate)
            silu_gate = own_gate * sigmoid_gate
            slope = sigmoid_gate * (1.0 + own_gate * (1.0 - sigmoid_gate))
            return jnp.concatenate(
                [
                    (silu_gate * own_up).astype(BF16),
                    (hidden_grad * own_up * slope).astype(BF16),
                    (hidden_grad * silu_gate).astype(BF16),
                ],
                axis=-1,
            )

        def gather_stage(w, stage):
            owns = activated(w) if stage == 0 else collected(w, stage - 1)
            live["own", w] = owns
            live["came", w] = [swap(own, order[-1 - stage]) for own, order in zip(owns, orders)]

        def collected(w, stage):
            return [
                jnp.concatenate([own, came], axis=order[-1 - stage] - 1)
                for own, came, order in zip(live.pop(("own", w)), live.pop(("came", w)), orders)
            ]

        def core_gather(w):
            owns = collected(w, stages - 1)
            live["mine", w] = owns
            live["other", w] = [swap(own, 0) for own in owns]

        def outputs(w):
            pieces = [
                piece.reshape(split, 3 * width)
                for both in zip(live.pop(("mine", w)), live.pop(("other", w)))
                for piece in both
            ]
            full = [
                jnp.concatenate([p[:, i * width : (i + 1) * width] for p in pieces], axis=0)
                for i in range(3)
            ]
            live["full", w] = full
            hidden, gate_grad, up_grad = full
            out_part = jnp.dot(hidden, down_weight, preferred_element_type=F32)
            in_part = contract_last(gate_grad, gate_weight) + contract_last(up_grad, up_weight)
            for s, k in enumerate(members(w)):
                parts = [p[s * 2 * split : (s + 1) * 2 * split] for p in (out_part, in_part)]
                if k:
                    parts = [shift(p.astype(BF16), -k) for p in parts]
                back[k] = parts

        def settle(pinned):
            nonlocal live
            names = list(live)
            values, arrived = lax.optimization_barrier(
                ([live[n] for n in names], [(tokens_at[k], grads_at[k]) for k in pinned])
            )
            live = dict(zip(names, values))
            for k, (part, grad) in zip(pinned, arrived):
                tokens_at[k], grads_at[k] = part, grad

        plan, pins = {}, {}
        for w in range(waves):
            first = 1 + stages * w
            for stage in range(stages):
                plan.setdefault(first + stage, []).append((1, reduce_stage, (w, stage)))
                plan.setdefault(first + stages + stage, []).append((0, gather_stage, (w, stage)))
            plan.setdefault(first - 1, []).append((3, products, (w,)))
            plan.setdefault(first + 2 * stages, []).append((2, core_gather, (w,)))
            plan.setdefault(first + 2 * stages + 1, []).append((4, outputs, (w,)))
            pins[first - 2] = members(w)
        for slot in range(max(plan) + 1):
            for _, work, args in sorted(plan[slot], key=lambda item: item[0]):
                work(*args)
            settle(pins.get(slot, []))

        token_panel = jnp.concatenate([tokens_at[k] for k in range(cols)], axis=0)
        grad_panel = jnp.concatenate([grads_at[k] for k in range(cols)], axis=0)
        hidden, gate_grad, up_grad = (
            jnp.concatenate([live["full", w][i] for w in range(waves)], axis=0) for i in range(3)
        )
        grads = (
            contract_first(token_panel, gate_grad).astype(BF16),
            contract_first(token_panel, up_grad).astype(BF16),
            contract_first(hidden, grad_panel).astype(BF16),
        )
        out_sum, in_sum = back[0]
        for k in range(1, cols):
            out_sum, in_sum = out_sum + back[k][0].astype(F32), in_sum + back[k][1].astype(F32)
        return (relative(out_sum.astype(BF16)), relative(in_sum.astype(BF16))) + grads

    return jax.shard_map(
        local,
        mesh=mesh,
        in_specs=(P("col", "row"), P("col", "row"), P("row", "col"), P("row", "col"), P("col", "row")),
        out_specs=(P("col", "row"), P("col", "row"), P("row", "col"), P("row", "col"), P("col", "row")),
        check_vma=False,
    )
```

```python
import jax
import jax.numpy as jnp
from jax import lax
from jax.sharding import PartitionSpec as P

F32 = jnp.float32
BF16 = jnp.bfloat16


def contract_last(left, right):
    return lax.dot_general(left, right, (((1,), (1,)), ((), ())), preferred_element_type=F32)


def contract_first(left, right):
    return lax.dot_general(left, right, (((0,), (0,)), ((), ())), preferred_element_type=F32)


def solution(mesh):
    rows, cols = mesh.shape["row"], mesh.shape["col"]
    bits = rows.bit_length() - 1

    def swap(block, bit):
        return lax.ppermute(block, "row", [(i, i ^ (1 << bit)) for i in range(rows)])

    def shift(block, by):
        return lax.ppermute(block, "col", [(i, (i + by) % cols) for i in range(cols)])

    def half(block, axis, side):
        return lax.slice_in_dim(block, side, side + 1, axis=axis)

    def blocked(panel):
        return panel.reshape((2,) * bits + (panel.shape[0] // rows, panel.shape[1]))

    def relative(panel):
        me = lax.axis_index("row")
        block = blocked(panel)
        for bit in range(bits):
            block = jnp.where((me >> bit) & 1 == 1, jnp.flip(block, bit), block)
        return block.reshape(panel.shape)

    def local(tokens, cotangent, gate_weight, up_weight, down_weight):
        width = gate_weight.shape[1]
        orders = [list(range(1, bits)), list(range(bits - 1, 0, -1))]
        stages, waves, pair = bits - 1, cols // 2, 2
        tokens_at, grads_at = {0: relative(tokens)}, {0: relative(cotangent)}
        for k in range(1, cols):
            grads_at[k] = shift(grads_at[k - 1], 1)
            tokens_at[k] = shift(tokens_at[k - 1], 1)
        live, back = {}, {}
        split = tokens.shape[0] // 2

        def members(w):
            return [pair * w + s for s in range(pair)]

        def products(w):
            def sums(low, high):
                part = jnp.concatenate([tokens_at[k][low:high] for k in members(w)], axis=0)
                grad = jnp.concatenate([grads_at[k][low:high] for k in members(w)], axis=0)
                return [
                    contract_last(grad, down_weight),
                    jnp.dot(part, gate_weight, preferred_element_type=F32),
                    jnp.dot(part, up_weight, preferred_element_type=F32),
                ]

            live["core_in", w] = [swap(s, 0) for s in sums(split, 2 * split)]
            live["core_keep", w] = sums(0, split)

        def partial(w, s, sides):
            def cut(block, done):
                for stage in range(done, len(sides)):
                    block = half(block, orders[s][stage] - 1, sides[stage])
                return block

            shape = (pair,) + (2,) * (bits - 1) + (2 * split // rows, width)
            values = []
            for i in range(3):
                value = cut(live["core_in", w][i].reshape(shape)[s], 0)
                value = value + cut(live["core_keep", w][i].reshape(shape)[s], 0)
                for stage, side in enumerate(sides):
                    if side == 0:
                        came = live["arrived", w, stage][s][..., i * width : (i + 1) * width]
                        value = value + cut(came, stage + 1).astype(F32)
                values.append(value)
            return values

        def reduce_stage(w, stage):
            arrived = []
            for s, order in enumerate(orders):
                sides = [0] * stage + [1]
                sent = [v.astype(BF16) for v in partial(w, s, sides)]
                arrived.append(swap(jnp.concatenate(sent, axis=-1), order[stage]))
            live["arrived", w, stage] = arrived

        def activated(w):
            owns = [activate(partial(w, s, [0] * stages)) for s in range(pair)]
            for name in [("core_in", w), ("core_keep", w)] + [("arrived", w, q) for q in range(stages)]:
                live.pop(name)
            return owns

        def activate(total):
            hidden_grad, own_gate, own_up = total
            sigmoid_gate = jax.nn.sigmoid(own_gate)
            silu_gate = own_gate * sigmoid_gate
            slope = sigmoid_gate * (1.0 + own_gate * (1.0 - sigmoid_gate))
            return jnp.concatenate(
                [
                    (silu_gate * own_up).astype(BF16),
                    (hidden_grad * own_up * slope).astype(BF16),
                    (hidden_grad * silu_gate).astype(BF16),
                ],
                axis=-1,
            )

        def gather_stage(w, stage):
            owns = activated(w) if stage == 0 else collected(w, stage - 1)
            live["own", w] = owns
            live["came", w] = [swap(own, order[-1 - stage]) for own, order in zip(owns, orders)]

        def collected(w, stage):
            return [
                jnp.concatenate([own, came], axis=order[-1 - stage] - 1)
                for own, came, order in zip(live.pop(("own", w)), live.pop(("came", w)), orders)
            ]

        def core_gather(w):
            owns = collected(w, stages - 1)
            live["mine", w] = owns
            live["other", w] = [swap(own, 0) for own in owns]

        def outputs(w):
            pieces = [
                piece.reshape(split, 3 * width)
                for both in zip(live.pop(("mine", w)), live.pop(("other", w)))
                for piece in both
            ]
            full = [
                jnp.concatenate([p[:, i * width : (i + 1) * width] for p in pieces], axis=0)
                for i in range(3)
            ]
            live["full", w] = full
            hidden, gate_grad, up_grad = full
            out_part = jnp.dot(hidden, down_weight, preferred_element_type=F32)
            in_part = contract_last(gate_grad, gate_weight) + contract_last(up_grad, up_weight)
            for s, k in enumerate(members(w)):
                parts = [p[s * 2 * split : (s + 1) * 2 * split] for p in (out_part, in_part)]
                if k:
                    parts = [shift(p.astype(BF16), -k) for p in parts]
                back[k] = parts

        def settle(pinned):
            nonlocal live
            names = list(live)
            values, arrived = lax.optimization_barrier(
                ([live[n] for n in names], [(tokens_at[k], grads_at[k]) for k in pinned])
            )
            live = dict(zip(names, values))
            for k, (part, grad) in zip(pinned, arrived):
                tokens_at[k], grads_at[k] = part, grad

        plan, pins = {}, {}
        for w in range(waves):
            first = 1 + stages * w
            for stage in range(stages):
                plan.setdefault(first + stage, []).append((1, reduce_stage, (w, stage)))
                plan.setdefault(first + stages + stage, []).append((0, gather_stage, (w, stage)))
            plan.setdefault(first - 1, []).append((3, products, (w,)))
            plan.setdefault(first + 2 * stages, []).append((2, core_gather, (w,)))
            plan.setdefault(first + 2 * stages + 1, []).append((4, outputs, (w,)))
            pins[first - 3] = pins.get(first - 3, []) + members(w)[:1]
            pins[first - 2] = pins.get(first - 2, []) + members(w)
        for slot in range(max(plan) + 1):
            for _, work, args in sorted(plan[slot], key=lambda item: item[0]):
                work(*args)
            settle(pins.get(slot, []))

        token_panel = jnp.concatenate([tokens_at[k] for k in range(cols)], axis=0)
        grad_panel = jnp.concatenate([grads_at[k] for k in range(cols)], axis=0)
        hidden, gate_grad, up_grad = (
            jnp.concatenate([live["full", w][i] for w in range(waves)], axis=0) for i in range(3)
        )
        grads = (
            contract_first(token_panel, gate_grad).astype(BF16),
            contract_first(token_panel, up_grad).astype(BF16),
            contract_first(hidden, grad_panel).astype(BF16),
        )
        out_sum, in_sum = back[0]
        for k in range(1, cols):
            out_sum, in_sum = out_sum + back[k][0].astype(F32), in_sum + back[k][1].astype(F32)
        return (relative(out_sum.astype(BF16)), relative(in_sum.astype(BF16))) + grads

    return jax.shard_map(
        local,
        mesh=mesh,
        in_specs=(P("col", "row"), P("col", "row"), P("row", "col"), P("row", "col"), P("col", "row")),
        out_specs=(P("col", "row"), P("col", "row"), P("row", "col"), P("row", "col"), P("col", "row")),
        check_vma=False,
    )
```

```python
import jax
import jax.numpy as jnp
from jax import lax
from jax.sharding import PartitionSpec as P

F32 = jnp.float32
BF16 = jnp.bfloat16


def contract_last(left, right):
    return lax.dot_general(left, right, (((1,), (1,)), ((), ())), preferred_element_type=F32)


def contract_first(left, right):
    return lax.dot_general(left, right, (((0,), (0,)), ((), ())), preferred_element_type=F32)


def solution(mesh):
    rows, cols = mesh.shape["row"], mesh.shape["col"]
    bits = rows.bit_length() - 1

    def swap(block, bit):
        return lax.ppermute(block, "row", [(i, i ^ (1 << bit)) for i in range(rows)])

    def shift(block, by):
        return lax.ppermute(block, "col", [(i, (i + by) % cols) for i in range(cols)])

    def half(block, axis, side):
        return lax.slice_in_dim(block, side, side + 1, axis=axis)

    def blocked(panel):
        return panel.reshape((2,) * bits + (panel.shape[0] // rows, panel.shape[1]))

    def relative(panel):
        me = lax.axis_index("row")
        block = blocked(panel)
        for bit in range(bits):
            block = jnp.where((me >> bit) & 1 == 1, jnp.flip(block, bit), block)
        return block.reshape(panel.shape)

    def local(tokens, cotangent, gate_weight, up_weight, down_weight):
        width = gate_weight.shape[1]
        orders = [list(range(1, bits)), list(range(bits - 1, 0, -1))]
        stages, waves, pair = bits - 1, cols // 2, 2
        tokens_at, grads_at = {0: relative(tokens)}, {0: relative(cotangent)}
        for k in range(1, cols):
            base, by = (k - 1, 1) if k < cols - 1 else (0, k)
            grads_at[k] = shift(grads_at[base], by)
            tokens_at[k] = shift(tokens_at[base], by)
        live, back = {}, {}
        split = tokens.shape[0] // 2

        def members(w):
            return [pair * w + s for s in range(pair)]

        def products(w):
            def sums(low, high):
                part = jnp.concatenate([tokens_at[k][low:high] for k in members(w)], axis=0)
                grad = jnp.concatenate([grads_at[k][low:high] for k in members(w)], axis=0)
                return [
                    contract_last(grad, down_weight),
                    jnp.dot(part, gate_weight, preferred_element_type=F32),
                    jnp.dot(part, up_weight, preferred_element_type=F32),
                ]

            live["core_in", w] = [swap(s, 0) for s in sums(split, 2 * split)]
            live["core_keep", w] = sums(0, split)

        def partial(w, s, sides):
            def cut(block, done):
                for stage in range(done, len(sides)):
                    block = half(block, orders[s][stage] - 1, sides[stage])
                return block

            shape = (pair,) + (2,) * (bits - 1) + (2 * split // rows, width)
            values = []
            for i in range(3):
                value = cut(live["core_in", w][i].reshape(shape)[s], 0)
                value = value + cut(live["core_keep", w][i].reshape(shape)[s], 0)
                for stage, side in enumerate(sides):
                    if side == 0:
                        came = live["arrived", w, stage][s][..., i * width : (i + 1) * width]
                        value = value + cut(came, stage + 1).astype(F32)
                values.append(value)
            return values

        def reduce_stage(w, stage):
            arrived = []
            for s, order in enumerate(orders):
                sides = [0] * stage + [1]
                sent = [v.astype(BF16) for v in partial(w, s, sides)]
                arrived.append(swap(jnp.concatenate(sent, axis=-1), order[stage]))
            live["arrived", w, stage] = arrived

        def activated(w):
            owns = [activate(partial(w, s, [0] * stages)) for s in range(pair)]
            for name in [("core_in", w), ("core_keep", w)] + [("arrived", w, q) for q in range(stages)]:
                live.pop(name)
            return owns

        def activate(total):
            hidden_grad, own_gate, own_up = total
            sigmoid_gate = jax.nn.sigmoid(own_gate)
            silu_gate = own_gate * sigmoid_gate
            slope = sigmoid_gate * (1.0 + own_gate * (1.0 - sigmoid_gate))
            return jnp.concatenate(
                [
                    (silu_gate * own_up).astype(BF16),
                    (hidden_grad * own_up * slope).astype(BF16),
                    (hidden_grad * silu_gate).astype(BF16),
                ],
                axis=-1,
            )

        def gather_stage(w, stage):
            owns = activated(w) if stage == 0 else collected(w, stage - 1)
            live["own", w] = owns
            live["came", w] = [swap(own, order[-1 - stage]) for own, order in zip(owns, orders)]

        def collected(w, stage):
            return [
                jnp.concatenate([own, came], axis=order[-1 - stage] - 1)
                for own, came, order in zip(live.pop(("own", w)), live.pop(("came", w)), orders)
            ]

        def core_gather(w):
            owns = collected(w, stages - 1)
            live["mine", w] = owns
            live["other", w] = [swap(own, 0) for own in owns]

        def outputs(w):
            pieces = [
                piece.reshape(split, 3 * width)
                for both in zip(live.pop(("mine", w)), live.pop(("other", w)))
                for piece in both
            ]
            full = [
                jnp.concatenate([p[:, i * width : (i + 1) * width] for p in pieces], axis=0)
                for i in range(3)
            ]
            live["full", w] = full
            hidden, gate_grad, up_grad = full
            out_part = jnp.dot(hidden, down_weight, preferred_element_type=F32)
            in_part = contract_last(gate_grad, gate_weight) + contract_last(up_grad, up_weight)
            for s, k in enumerate(members(w)):
                parts = [p[s * 2 * split : (s + 1) * 2 * split] for p in (out_part, in_part)]
                if k:
                    parts = [shift(p.astype(BF16), -k) for p in parts]
                back[k] = parts

        def settle(pinned):
            nonlocal live
            names = list(live)
            values, arrived = lax.optimization_barrier(
                ([live[n] for n in names], [(tokens_at[k], grads_at[k]) for k in pinned])
            )
            live = dict(zip(names, values))
            for k, (part, grad) in zip(pinned, arrived):
                tokens_at[k], grads_at[k] = part, grad

        plan, pins = {}, {}
        for w in range(waves):
            first = 1 + stages * w
            for stage in range(stages):
                plan.setdefault(first + stage, []).append((1, reduce_stage, (w, stage)))
                plan.setdefault(first + stages + stage, []).append((0, gather_stage, (w, stage)))
            plan.setdefault(first - 1, []).append((3, products, (w,)))
            plan.setdefault(first + 2 * stages, []).append((2, core_gather, (w,)))
            plan.setdefault(first + 2 * stages + 1, []).append((4, outputs, (w,)))
        for slot in range(max(plan) + 1):
            for _, work, args in sorted(plan[slot], key=lambda item: item[0]):
                work(*args)
            settle(pins.get(slot, []))

        token_panel = jnp.concatenate([tokens_at[k] for k in range(cols)], axis=0)
        grad_panel = jnp.concatenate([grads_at[k] for k in range(cols)], axis=0)
        hidden, gate_grad, up_grad = (
            jnp.concatenate([live["full", w][i] for w in range(waves)], axis=0) for i in range(3)
        )
        grads = (
            contract_first(token_panel, gate_grad).astype(BF16),
            contract_first(token_panel, up_grad).astype(BF16),
            contract_first(hidden, grad_panel).astype(BF16),
        )
        out_sum, in_sum = back[0]
        for k in range(1, cols):
            out_sum, in_sum = out_sum + back[k][0].astype(F32), in_sum + back[k][1].astype(F32)
        return (relative(out_sum.astype(BF16)), relative(in_sum.astype(BF16))) + grads

    return jax.shard_map(
        local,
        mesh=mesh,
        in_specs=(P("col", "row"), P("col", "row"), P("row", "col"), P("row", "col"), P("col", "row")),
        out_specs=(P("col", "row"), P("col", "row"), P("row", "col"), P("row", "col"), P("col", "row")),
        check_vma=False,
    )
```
